32 devices in a mesh: row: 16 (over z, y, core), col: 2 (over x).
Axes of the slice: x: 2, y: 2, z: 4, core: 2. Of those that a mesh axis runs over, the one named last changes fastest.
Arguments:
- queries: bfloat16 [128, 64, 2240], P('row', 'col'), may hold values from -6 to 6
- keys: bfloat16 [128, 64, 2240], P('row', 'col'), may hold values from -120 to 120
- values: bfloat16 [128, 64, 2240], P('row', 'col'), may hold values from -10 to 10
- features: bfloat16 [128, 64, 11200], P('row', 'col'), may hold values from -6 to 6
- conv_weight: bfloat16 [3, 3, 11200], replicated, may hold values from -2 to 2
- conv_bias: bfloat16 [11200], replicated, may hold values from -3 to 3
Outputs:
- attended: bfloat16 [128, 64, 2240], P('row', 'col')
- gated: bfloat16 [128, 64, 5600], P('row', 'col')
The draws below stay inside these ranges and needn't reach their ends.
All inputs are finite; a program needn't handle non-finite values.
Results may differ from the reference program's by a relative error of at most 0.001.
Values may be sent and summed in bfloat16 or wider, within the bound.
No kernel may reach another device: no remote copies, remote signals or barrier semaphores. Data moves between devices by JAX's collectives and lax.ppermute only.
A program may use at most 128 MiB of HBM per device.

```python
import math
import jax
import jax.numpy as jnp
from jax import lax

D = 2240
HEADS = 70
HEAD_DIM = 32
HID = 5600
TILE_R = 8
TILE_C = 32
IMG_H = 128
IMG_W = 64


def draw_keys(key, part):
    noise_key, scale_key = jax.random.split(key, 2)
    pick_key = jax.random.fold_in(key, 77)
    full_shape = (IMG_H, IMG_W, D)
    tile_count = IMG_H // TILE_R * (IMG_W // TILE_C)
    strong_tile = jax.random.randint(pick_key, (), 0, tile_count)
    tile_index = (jnp.arange(IMG_H, dtype=jnp.int32) // TILE_R).reshape(IMG_H, 1, 1) * (IMG_W // TILE_C) + (jnp.arange(IMG_W, dtype=jnp.int32) // TILE_C).reshape(1, IMG_W, 1)
    tile_weight = jnp.where(tile_index == strong_tile, 1.0, 0.02).astype(jnp.float32)
    row_place = jnp.arange(IMG_H, dtype=jnp.float32).reshape(IMG_H, 1, 1) / (IMG_H - 1)
    noise_part = jnp.clip(jax.random.normal(noise_key, full_shape, jnp.float32), -6.0, 6.0)
    row_rise = 1.0 + 2.0 * row_place
    magnitude = jnp.exp(jax.random.uniform(scale_key, (IMG_H, IMG_W, 1), jnp.float32) * math.log(10.0))
    return (noise_part * magnitude * row_rise * tile_weight / 3.0).astype(jnp.bfloat16)


def draw_values(key, part):
    mean_key, shift_key, noise_key = jax.random.split(key, 3)
    full_shape = (IMG_H, IMG_W, D)
    channel_mean = jnp.clip(jax.random.normal(mean_key, (D,), jnp.float32), -3.0, 3.0)
    tile_shift = jnp.clip(jax.random.normal(shift_key, (IMG_H // TILE_R, IMG_W // TILE_C, D), jnp.float32), -3.0, 3.0)
    tile_shift = jnp.repeat(jnp.repeat(tile_shift, TILE_R, axis=0), TILE_C, axis=1)
    noise_part = jnp.clip(jax.random.normal(noise_key, full_shape, jnp.float32), -4.0, 4.0)
    result = channel_mean + tile_shift + noise_part
    return result.astype(jnp.bfloat16)


def shard_levels(own_key, shape, cuts, smallest, top_value):
    loudness = 1.0
    for position, parts in cuts:
        draws = jax.random.uniform(jax.random.fold_in(jax.random.fold_in(own_key, 6), position), (parts,), jnp.float32, smallest / len(cuts), top_value / len(cuts))
        loudness = loudness * jnp.repeat(jnp.exp(draws), shape[position] // parts).reshape((-1,) + (1,) * (len(shape) - 1 - position))
    return loudness


def scatter_about(own_key, shape, scale, limit, shards=(), held_as=jnp.bfloat16):
    drawn = jax.random.normal(own_key, shape, jnp.float32) * scale
    if len(shards) > 0:
        drawn = shard_levels(own_key, shape, shards, -0.22, 0.18) * drawn
    return jnp.clip(drawn, min=-limit, max=limit).astype(held_as)


def setup_inputs(seed: int = 0) -> dict:
    seeds = jax.random.split(jax.random.key(seed), 7)
    queries = scatter_about(seeds[0], (IMG_H, IMG_W, D), 1.0, 6.0, ((0, 16), (1, 2)))
    keys = draw_keys(jax.random.fold_in(seeds[6], 71), 0)
    values = draw_values(jax.random.fold_in(seeds[6], 71), 0)
    features = scatter_about(seeds[3], (IMG_H, IMG_W, 2 * HID), 1.0, 6.0, ((0, 16), (1, 2)))
    conv_weight = scatter_about(seeds[4], (3, 3, 2 * HID), 9 ** -0.5, 2.0)
    conv_bias = scatter_about(seeds[5], (2 * HID,), 0.5, 3.0)
    return dict(queries=queries, keys=keys, values=values, features=features, conv_weight=conv_weight, conv_bias=conv_bias)


def reference(queries, keys, values, features, conv_weight, conv_bias):
    def add_row(running, row_pair):
        key_row, value_row = row_pair
        key_heads = jnp.maximum(key_row.astype(jnp.float32), 0.0).reshape(-1, HEADS, HEAD_DIM)
        value_heads = value_row.astype(jnp.float32).reshape(-1, HEADS, HEAD_DIM)
        kv_sum, key_sum = running
        kv_sum = kv_sum + jnp.einsum("thj,thi->jhi", value_heads, key_heads)
        key_sum = key_sum + jnp.sum(key_heads, axis=0)
        return (kv_sum, key_sum), None

    initial = (jnp.zeros((HEAD_DIM, HEADS, HEAD_DIM), jnp.float32), jnp.zeros((HEADS, HEAD_DIM), jnp.float32))
    (kv_state, key_total), ignored = lax.scan(add_row, initial, (keys, values))

    def attend_row(query_row):
        query_heads = jnp.maximum(query_row.astype(jnp.float32), 0.0).reshape(-1, HEADS, HEAD_DIM)
        numerator = jnp.einsum("thi,jhi->thj", query_heads, kv_state, precision=lax.Precision.HIGHEST)
        denominator = jnp.einsum("thi,hi->th", query_heads, key_total, precision=lax.Precision.HIGHEST)
        return (numerator / (denominator[:, :, None] + 1e-15)).astype(jnp.bfloat16).reshape(IMG_W, D)

    attended = lax.map(attend_row, queries)

    padded = jnp.pad(features, ((1, 1), (1, 1), (0, 0)))
    weight_float = conv_weight.astype(jnp.float32)
    bias_float = conv_bias.astype(jnp.float32)

    def conv_row(row_index):
        band_rows = lax.dynamic_slice_in_dim(padded, row_index, 3, 0).astype(jnp.float32)
        conv_sum = bias_float
        for tap_row in range(3):
            for tap_col in range(3):
                conv_sum = conv_sum + weight_float[tap_row, tap_col] * band_rows[tap_row, tap_col:tap_col + IMG_W]
        return (conv_sum[:, :HID] * jax.nn.silu(conv_sum[:, HID:])).astype(jnp.bfloat16)

    gated = lax.map(conv_row, jnp.arange(IMG_H, dtype=jnp.int32))
    return attended, gated
```

```python
import functools
import jax
import jax.numpy as jnp
from jax import lax
from jax.experimental import pallas as pl
from jax.experimental.pallas import tpu as pltpu
from jax.sharding import PartitionSpec as P

HEAD_DIM = 32
LANES = 128
WIDE = 768
PAIR = 256
SUBLANES = 16
SMALL = pl.CostEstimate(flops=1024, bytes_accessed=1024, transcendentals=0)


def halves(channels):
    tiles = pl.cdiv(channels, LANES)
    per = pl.cdiv(tiles, 2)
    return tiles, per, pl.cdiv(per * (HEAD_DIM + 1), 8) * 8


def same_head(size):
    row_head = lax.broadcasted_iota(jnp.int32, (size, size), 0) // HEAD_DIM
    col_head = lax.broadcasted_iota(jnp.int32, (size, size), 1) // HEAD_DIM
    return row_head == col_head


def state_kernel(channels, place, k_ref, v_ref, features, mine, other, far, *refs):
    edge, *refs = refs if len(refs) == 5 else (None, *refs)
    packed, row, *refs = refs
    beside, sem = refs if len(refs) == 2 else (None, *refs)
    tiles, per, rows = halves(channels)
    step = pl.program_id(0)
    core = place[0]
    tokens = k_ref.shape[0] * k_ref.shape[1]
    tile_rows, tile_cols, width = features.shape
    copies = [pltpu.make_async_copy(features.at[(tile_rows - 1) * core], row, sem.at[0])]
    store = pltpu.make_async_copy(row, far.at[0], sem.at[1])
    if edge is not None:
        start = pl.multiple_of((tile_cols - SUBLANES) * (1 - place[1]), SUBLANES)
        copies.append(
            pltpu.make_async_copy(features.at[:, pl.ds(start, SUBLANES)], beside, sem.at[2])
        )

    @pl.when(step == 0)
    def _():
        for copy in copies:
            copy.start()
        packed[...] = jnp.zeros_like(packed)

    mask = same_head(PAIR)
    ones = jnp.ones((8, tokens), jnp.bfloat16)
    for part in range(WIDE // PAIR):
        at = slice(part * PAIR, (part + 1) * PAIR)
        keys = jnp.maximum(k_ref[:, :, at].reshape(tokens, PAIR), 0)
        values = v_ref[:, :, at].reshape(tokens, PAIR)
        product = lax.dot_general(
            values, keys, (((0,), (0,)), ((), ())), preferred_element_type=jnp.float32
        )
        product = jnp.where(mask, product, 0.0)
        state = product[:HEAD_DIM]
        for head in range(1, PAIR // HEAD_DIM):
            state = state + product[head * HEAD_DIM : (head + 1) * HEAD_DIM]
        total = jnp.dot(ones, keys, preferred_element_type=jnp.float32)
        for side in range(PAIR // LANES):
            tile = (step * (WIDE // PAIR) + part) * (PAIR // LANES) + side
            lanes = slice(side * LANES, (side + 1) * LANES)

            @pl.when(tile < tiles)
            def _():
                half, spot = tile // per, tile % per
                begin = pl.multiple_of(spot * HEAD_DIM, HEAD_DIM)
                packed[half, pl.ds(begin, HEAD_DIM), :] = state[:, lanes]
                packed[half, pl.ds(per * HEAD_DIM + spot, 1), :] = total[:1, lanes]

    @pl.when(step == pl.num_programs(0) - 1)
    def _():
        mine[...] = packed[core]
        other[...] = packed[1 - core]

        store.wait()

    @pl.when(step == 1)
    def _():
        copies[0].wait()
        store.start()

    if edge is not None:

        @pl.when(step == 1)
        def _():
            copies[1].wait()

            @pl.when(place[1] == 0)
            def _():
                edge[...] = beside[:, SUBLANES - 1, :]

            @pl.when(place[1] != 0)
            def _():
                edge[...] = beside[:, 0, :]


def local_state(place, keys, values, features, with_edge):
    tile_rows, tile_cols, channels = keys.shape
    width = features.shape[2]
    rows = halves(channels)[2]
    block = pl.BlockSpec((tile_rows, tile_cols, WIDE), lambda i, c: (0, 0, i))
    shapes = [jax.ShapeDtypeStruct((rows, LANES), jnp.float32)] * 2
    scratch = [pltpu.VMEM((2, rows, LANES), jnp.float32)]
    shapes.append(pltpu.HBM((1, tile_cols, width), features.dtype))
    scratch.append(pltpu.VMEM((tile_cols, width), features.dtype))
    if with_edge:
        shapes.append(jax.ShapeDtypeStruct((tile_rows, width), features.dtype))
        scratch.append(pltpu.VMEM((tile_rows, SUBLANES, width), features.dtype))
    return pl.pallas_call(
        functools.partial(state_kernel, channels),
        out_shape=shapes,
        grid_spec=pltpu.PrefetchScalarGridSpec(
            num_scalar_prefetch=1,
            grid=(pl.cdiv(channels, WIDE),),
            in_specs=[block, block, pl.BlockSpec(memory_space=pl.ANY)],
            out_specs=[
                pl.BlockSpec(memory_space=pl.ANY if len(x.shape) == 3 else pltpu.VMEM) for x in shapes
            ],
            scratch_shapes=scratch + [pltpu.SemaphoreType.DMA((3,))],
        ),
        compiler_params=pltpu.CompilerParams(vmem_limit_bytes=8 << 20),
        cost_estimate=pl.CostEstimate(flops=1 << 29, bytes_accessed=64 << 20, transcendentals=0),
        name="local_state",
    )(place, *(pltpu.with_memory_space_constraint(x, pltpu.HBM) for x in (keys, values, features)))


def in_two(x):
    high = x.astype(jnp.bfloat16)
    return high, (x - high.astype(jnp.float32)).astype(jnp.bfloat16)


def attend_kernel(channels, place, q_ref, mine, other, ends, _, out, gated, packed, sem):
    tiles, per, rows = halves(channels)
    step = pl.program_id(0)
    core = place[0]
    tile_rows, tile_cols, _ = q_ref.shape
    tokens = tile_rows * tile_cols
    copies = [
        pltpu.make_async_copy(ends.at[k], gated.at[(tile_rows - 1) * low], sem.at[k])
        for k, low in enumerate((1 - core, core))
    ]

    @pl.when(step == 0)
    def _():
        for copy in copies:
            copy.start()
        packed[core] = mine[...]
        packed[1 - core] = other[...]

    mask = same_head(PAIR)
    lane = lax.broadcasted_iota(jnp.int32, (tokens, PAIR), 1)
    zero = jnp.zeros((), jnp.bfloat16)

    def weighted(queries, matrices):
        total = None
        for matrix in matrices:
            matrix = jnp.where(mask, matrix, zero)
            term = lax.dot_general(
                queries, matrix, (((1,), (1,)), ((), ())), preferred_element_type=jnp.float32
            )
            total = term if total is None else total + term
        return total

    for part in range(WIDE // PAIR):
        pair = step * (WIDE // PAIR) + part
        at = slice(part * PAIR, (part + 1) * PAIR)
        queries = jnp.maximum(q_ref[:, :, at].reshape(tokens, PAIR), 0)
        queries = jnp.where(lane < channels - pair * PAIR, queries, zero)
        states, totals = [], []
        for side in range(PAIR // LANES):
            tile = jnp.minimum(pair * (PAIR // LANES) + side, tiles - 1)
            half, place = tile // per, tile % per
            start = pl.multiple_of(place * HEAD_DIM, HEAD_DIM)
            states.append(packed[half, pl.ds(start, HEAD_DIM), :])
            totals.append(packed[half, pl.ds(per * HEAD_DIM + place, 1), :])
        state, total = jnp.concatenate(states, 1), jnp.concatenate(totals, 1)
        numerator = weighted(
            queries, [jnp.concatenate([x] * (PAIR // HEAD_DIM), 0) for x in in_two(state)]
        )
        denominator = weighted(queries, [jnp.broadcast_to(x, (PAIR, PAIR)) for x in in_two(total)])
        result = (numerator / (denominator + 1e-15)).astype(jnp.bfloat16)
        out[:, :, at] = result.reshape(tile_rows, tile_cols, PAIR)

    @pl.when(step == pl.num_programs(0) - 1)
    def _():
        for copy in copies:
            copy.wait()


def attend(place, queries, mine, other, ends, gated):
    tile_rows, tile_cols, channels = queries.shape
    rows = halves(channels)[2]
    block = pl.BlockSpec((tile_rows, tile_cols, WIDE), lambda i, c: (0, 0, i))
    half = pl.BlockSpec((rows, LANES), lambda i, c: (0, 0))
    anywhere = pl.BlockSpec(memory_space=pl.ANY)
    return pl.pallas_call(
        functools.partial(attend_kernel, channels),
        out_shape=[
            jax.ShapeDtypeStruct(x.shape, jnp.bfloat16) for x in (queries, gated)
        ],
        grid_spec=pltpu.PrefetchScalarGridSpec(
            num_scalar_prefetch=1,
            grid=(pl.cdiv(channels, WIDE),),
            in_specs=[block, half, half, pl.BlockSpec(memory_space=pltpu.VMEM), anywhere],
            out_specs=[block, anywhere],
            scratch_shapes=[
                pltpu.VMEM((2, rows, LANES), jnp.float32),
                pltpu.SemaphoreType.DMA((2,)),
            ],
        ),
        input_output_aliases={5: 1},
        compiler_params=pltpu.CompilerParams(vmem_limit_bytes=8 << 20),
        cost_estimate=SMALL,
        name="attend",
    )(place, queries, mine, other, ends, gated)


def widened(x):
    channel = lax.broadcasted_iota(jnp.int32, (1, x.shape[1]), 1)
    return x.astype(jnp.float32) * jnp.where(channel < x.shape[1] // 2, 1.0, 0.5)


def conv_kernel(targets, firsts, unroll, *refs):
    where, features, beside, *refs = refs
    if not targets:
        near, far, near_corner, far_corner, *refs = refs
        parts, refs = refs[: len(firsts)], refs[len(firsts) :]
        *refs, sem = refs
    weight, bias, out, *refs = refs
    copies = []
    if not targets:
        gated, *refs = refs
        for k, (start, part) in enumerate(zip(firsts, parts)):
            place = gated.at[pl.ds(start, part.shape[0])]
            copies.append(pltpu.make_async_copy(part, place, sem.at[k]))
            copies[-1].start()
    weights, biases, margins, sums, carry = refs
    tile_rows, tile_cols, channels = features.shape
    hidden = channels // 2
    tiles = pl.cdiv(hidden, LANES)
    first_gate = hidden // LANES
    shift = LANES - hidden % LANES
    count = len(targets) or 2
    last = tile_rows - 1
    core = where[0]
    if targets:
        first = targets[0] - 1
        sources = [(features, first + k) for k in range(count + 2)]
        triples = [(k, k + 1, k + 2) for k in range(count)]
        orders = [[0, 1, 2]] * count
    else:
        sources = [
            (near, 0), (features, (1 - core) * last), (features, 1 + (1 - core) * (last - 2)),
            (far, 0), (features, core * last), (features, 1 + core * (last - 2)),
        ]
        triples = [(0, 1, 2), (3, 4, 5)]
        orders = [[2 * (1 - core), 1, 2 * core], [2 * core, 1, 2 * (1 - core)]]

    for tap in range(3):
        weights[tap, :, :channels] = widened(weight[tap])
    biases[:, :channels] = widened(bias[...])
    for side in range(2):
        place = side * (beside.shape[0] - 1)
        keep = where[1 + side].astype(jnp.float32)
        edge = beside[place].astype(jnp.float32) * keep
        column = slice(2 * side, 2 * side + 1)
        if targets:
            rows = [edge[first + tap : first + tap + count] for tap in range(3)]
            margins[side, :, :channels] = sum(
                rows[tap] * weights[tap, column, :channels] for tap in range(3)
            )
            continue
        top = edge[:1], edge[1:2]
        bottom = edge[last:], edge[last - 1 : last]
        for target, corner in enumerate((near_corner, far_corner)):
            below = core == (1 if target else 0)
            rows = [corner[place : place + 1].astype(jnp.float32) * keep]
            rows += [jnp.where(below, low, high) for low, high in zip(bottom, top)]
            margins[side, target : target + 1, :channels] = sum(
                row * weights[tap, column, :channels] for row, tap in zip(rows, orders[target])
            )

    def span(tile):
        if isinstance(tile, int):
            return slice(tile * LANES, (tile + 1) * LANES)
        return pl.ds(pl.multiple_of(tile * LANES, LANES), LANES)

    def read(source, row, tile):
        if not isinstance(tile, int) or (tile + 1) * LANES <= channels:
            return source[row, :, span(tile)].astype(jnp.float32)
        part = source[row, :, tile * LANES :].astype(jnp.float32)
        fill = jnp.zeros((tile_cols, LANES - part.shape[1]), jnp.float32)
        return jnp.concatenate([part, fill], 1)

    def add_up(tile, buffer):
        at = span(tile)
        tokens = [read(source, row, tile) for source, row in sources]
        factors = [
            [[weights[tap, col : col + 1, at] for col in range(3)] for tap in order]
            for order in (orders[:1] if targets else orders)
        ]
        for target, triple in enumerate(triples):
            factor = factors[0 if targets else target]
            for col in (0, 2, 1):
                total = sum(factor[k][col] * tokens[triple[k]] for k in range(3))
                if col == 1:
                    total = total + biases[:, at]
                sums[buffer, target, col, 8 : 8 + tile_cols, :] = total
            sums[buffer, target, 0, 7:8, :] = margins[0, target : target + 1, at]
            sums[buffer, target, 2, 8 + tile_cols : 9 + tile_cols, :] = margins[1, target : target + 1, at]

    def collect(buffer, target):
        return (
            sums[buffer, target, 1, 8 : 8 + tile_cols, :]
            + sums[buffer, target, 0, 7 : 7 + tile_cols, :]
            + sums[buffer, target, 2, 9 : 9 + tile_cols, :]
        )

    def gate(buffer, target):
        x = collect(buffer, target)
        return pltpu.roll(x + x * jnp.tanh(x), shift, 1)

    lane = lax.broadcasted_iota(jnp.int32, (tile_cols, LANES), 1)

    def add_both(tile, step):
        add_up(tile + first_gate + 1, 2 * step)
        add_up(tile, 2 * step + 1)

    def finish(tile, step, before):
        at = span(tile)
        result = []
        for target in range(count):
            after = gate(2 * step, target)
            factor = jnp.where(lane < shift, before[target], after)
            product = (collect(2 * step + 1, target) * factor).astype(jnp.bfloat16)
            if isinstance(tile, int):
                size = min(hidden - tile * LANES, LANES)
                out[target, :, tile * LANES : tile * LANES + size] = product[:, :size]
            else:
                out[target, :, at] = product
            result.append(after)
        return result

    add_up(first_gate, 0)
    for target in range(count):
        carry[target] = gate(0, target)
    add_both(0, 0)

    full = tiles // unroll - 1

    @pl.loop(0, full)
    def _(i):
        before = [carry[target] for target in range(count)]
        for step in range(unroll):
            tile = i * unroll + step
            add_both(tile + 1, (step + 1) % unroll)
            before = finish(tile, step, before)
        for target in range(count):
            carry[target] = before[target]

    before = [carry[target] for target in range(count)]
    for tile in range(full * unroll, tiles):
        if tile + 1 < tiles:
            add_both(tile + 1, (tile + 1) % unroll)
        before = finish(tile, tile % unroll, before)

    for copy in copies:
        copy.wait()


def conv(targets, where, features, beside, halos, parts, firsts, weight, bias):
    tile_rows, tile_cols, channels = features.shape
    hidden = channels // 2
    count = len(targets) or 2
    unroll = 2 if targets else 4
    padded = pl.cdiv(channels, LANES) * LANES
    whole = pl.BlockSpec(memory_space=pltpu.VMEM)
    operands = [features, beside, *halos, *parts, weight, bias]
    shapes = [jax.ShapeDtypeStruct((count, tile_cols, hidden), jnp.bfloat16)]
    specs = [whole]
    scratch = [
        pltpu.VMEM((3, 3, padded), jnp.float32),
        pltpu.VMEM((1, padded), jnp.float32),
        pltpu.VMEM((2, count, padded), jnp.float32),
        pltpu.VMEM((2 * unroll, count, 3, tile_cols + 16, LANES), jnp.float32),
        pltpu.VMEM((count, tile_cols, LANES), jnp.float32),
    ]
    if not targets:
        shapes.append(jax.ShapeDtypeStruct((tile_rows, tile_cols, hidden), jnp.bfloat16))
        specs.append(pl.BlockSpec(memory_space=pl.ANY))
        scratch.append(pltpu.SemaphoreType.DMA((len(parts),)))
    return pl.pallas_call(
        functools.partial(conv_kernel, targets, firsts, unroll),
        out_shape=shapes,
        in_specs=[pl.BlockSpec(memory_space=pltpu.SMEM)] + [whole] * len(operands),
        out_specs=specs,
        scratch_shapes=scratch,
        compiler_params=pltpu.CompilerParams(vmem_limit_bytes=8 << 20),
        cost_estimate=SMALL,
        name="conv_rows" if targets else "conv_ends",
    )(where, *operands)


def near_kernel(place, features, near, sem):
    row = (features.shape[0] - 1) * (1 - place[0])
    copy = pltpu.make_async_copy(features.at[pl.ds(row, 1)], near, sem)
    copy.start()
    copy.wait()


def near_row(place, features):
    return pl.pallas_call(
        near_kernel,
        out_shape=pltpu.HBM((1, *features.shape[1:]), features.dtype),
        in_specs=[pl.BlockSpec(memory_space=pltpu.SMEM), pl.BlockSpec(memory_space=pltpu.VMEM)],
        out_specs=pl.BlockSpec(memory_space=pl.ANY),
        scratch_shapes=[pltpu.SemaphoreType.DMA],
        compiler_params=pltpu.CompilerParams(vmem_limit_bytes=8 << 20),
        cost_estimate=SMALL,
        name="near_row",
    )(place, features)


def swap(axis, bit):
    return [(i, i ^ bit) for i in range(lax.axis_size(axis))]


def together(*values):
    return lax.optimization_barrier(values)


def on_device(queries, keys, values, features, conv_weight, conv_bias):
    tile_rows, tile_cols, channels = features.shape
    rows, cols = lax.axis_size("row"), lax.axis_size("col")
    row, col = lax.axis_index("row"), lax.axis_index("col")
    core = (row % 2).astype(jnp.int32)
    place = jnp.stack([core, col]).astype(jnp.int32)
    where = jnp.stack([core, col > 0, col < cols - 1]).astype(jnp.int32)
    bias = conv_bias.reshape(1, -1)
    next_chip = [(i, i + 1) for i in range(1, rows - 1, 2)]
    next_chip += [(i + 1, i) for i, _ in next_chip]

    mine, other, far, *edges = local_state(place, keys, values, features, cols == 2)
    total = mine + lax.ppermute(other, "row", swap("row", 1))
    if cols == 2:
        beside = lax.ppermute(edges[0], "col", swap("col", 1))[None]
    else:
        right = [(i, i + 1) for i in range(cols - 1)]
        left = [(i + 1, i) for i in range(cols - 1)]
        beside = jnp.stack(
            [
                lax.ppermute(features[:, -1], "col", right),
                lax.ppermute(features[:, 0], "col", left),
            ]
        )
    rounds = [("row", 1 << k) for k in range(2, (rows - 1).bit_length())]
    rounds[1:1] = [("col", 1 << k) for k in range((cols - 1).bit_length())]
    rounds.append(("row", 2))
    mixed = {0: (4, 2), len(rounds) - 1: (2, 4)}
    middle = min(3, tile_rows - 1)
    work = [tuple(range(1, middle)), tuple(range(middle, tile_rows - 1)), ()]
    firsts, parts = [], []

    def next_work(given):
        targets = work.pop(0)
        halos = () if targets else (near_halo, far_halo, near_corner, far_corner)
        earlier = () if targets else tuple(parts)
        made = list(
            conv(targets, given, features, beside, halos, earlier, tuple(firsts), conv_weight, bias)
        )
        if not targets:
            return made
        firsts.append(targets[0])
        parts.extend(made)
        return made

    for turn, (axis, bit) in enumerate(rounds):
        pairs = swap(axis, bit)
        if turn in mixed:
            pairs = [(i, i ^ mixed[turn][i % 2]) for i in range(rows)]
        received = lax.ppermute(total, axis, pairs)
        if turn == 0:
            far_halo = lax.ppermute(together(far, total)[0], "row", next_chip)
            near = near_row(together(place, total)[0], features)
            received, near, beside = together(received, near, beside)
            near_halo = lax.ppermute(near, "row", swap("row", 1))
            near_corner = jnp.where(core == 0, beside[:, -1], beside[:, 0])
            far_corner = jnp.where(core == 0, beside[:, 0], beside[:, -1])
            near_corner = lax.ppermute(near_corner, "row", swap("row", 1))
            far_corner = lax.ppermute(far_corner, "row", next_chip)
        if turn == 1:
            received, near_halo, near_corner = together(received, near_halo, near_corner)
        if turn > 0 and work:
            made = next_work(together(where, total)[0])
            received, made[0] = together(received, made[0])
            if work:
                parts[-1] = made[0]
        if turn == 2:
            received, far_halo, far_corner = together(received, far_halo, far_corner)
        total = total + received
    rest = lax.ppermute(total, "row", swap("row", 1))
    while work:
        made = next_work(where)
    return tuple(attend(place, queries, total, rest, *made))


def solution(mesh):
    tiled = P("row", "col", None)
    return jax.shard_map(
        on_device,
        mesh=mesh,
        in_specs=(tiled, tiled, tiled, tiled, P(), P()),
        out_specs=(tiled, tiled),
        check_vma=False,
    )
```

```python
import functools
import jax
import jax.numpy as jnp
from jax import lax
from jax.experimental import pallas as pl
from jax.experimental.pallas import tpu as pltpu
from jax.sharding import PartitionSpec as P

HEAD_DIM = 32
LANES = 128
WIDE = 768
PAIR = 256
SUBLANES = 16
SMALL = pl.CostEstimate(flops=1024, bytes_accessed=1024, transcendentals=0)


def halves(channels):
    tiles = pl.cdiv(channels, LANES)
    per = pl.cdiv(tiles, 2)
    return tiles, per, pl.cdiv(per * (HEAD_DIM + 1), 8) * 8


def same_head(size):
    row_head = lax.broadcasted_iota(jnp.int32, (size, size), 0) // HEAD_DIM
    col_head = lax.broadcasted_iota(jnp.int32, (size, size), 1) // HEAD_DIM
    return row_head == col_head


def state_kernel(channels, place, k_ref, v_ref, features, mine, other, far, *refs):
    edge, *refs = refs if len(refs) == 5 else (None, *refs)
    packed, row, *refs = refs
    beside, sem = refs if len(refs) == 2 else (None, *refs)
    tiles, per, rows = halves(channels)
    step = pl.program_id(0)
    core = place[0]
    tokens = k_ref.shape[0] * k_ref.shape[1]
    tile_rows, tile_cols, width = features.shape
    copies = [pltpu.make_async_copy(features.at[(tile_rows - 1) * core], row, sem.at[0])]
    store = pltpu.make_async_copy(row, far.at[0], sem.at[1])
    if edge is not None:
        start = pl.multiple_of((tile_cols - SUBLANES) * (1 - place[1]), SUBLANES)
        copies.append(
            pltpu.make_async_copy(features.at[:, pl.ds(start, SUBLANES)], beside, sem.at[2])
        )

    @pl.when(step == 0)
    def _():
        for copy in copies:
            copy.start()
        packed[...] = jnp.zeros_like(packed)

    mask = same_head(PAIR)
    ones = jnp.ones((8, tokens), jnp.bfloat16)
    for part in range(WIDE // PAIR):
        at = slice(part * PAIR, (part + 1) * PAIR)
        keys = jnp.maximum(k_ref[:, :, at].reshape(tokens, PAIR), 0)
        values = v_ref[:, :, at].reshape(tokens, PAIR)
        product = lax.dot_general(
            values, keys, (((0,), (0,)), ((), ())), preferred_element_type=jnp.float32
        )
        product = jnp.where(mask, product, 0.0)
        state = product[:HEAD_DIM]
        for head in range(1, PAIR // HEAD_DIM):
            state = state + product[head * HEAD_DIM : (head + 1) * HEAD_DIM]
        total = jnp.dot(ones, keys, preferred_element_type=jnp.float32)
        for side in range(PAIR // LANES):
            tile = (step * (WIDE // PAIR) + part) * (PAIR // LANES) + side
            lanes = slice(side * LANES, (side + 1) * LANES)

            @pl.when(tile < tiles)
            def _():
                half, spot = tile // per, tile % per
                begin = pl.multiple_of(spot * HEAD_DIM, HEAD_DIM)
                packed[half, pl.ds(begin, HEAD_DIM), :] = state[:, lanes]
                packed[half, pl.ds(per * HEAD_DIM + spot, 1), :] = total[:1, lanes]

    @pl.when(step == pl.num_programs(0) - 1)
    def _():
        mine[...] = packed[core]
        other[...] = packed[1 - core]

        store.wait()

    @pl.when(step == 1)
    def _():
        copies[0].wait()
        store.start()

    if edge is not None:

        @pl.when(step == 1)
        def _():
            copies[1].wait()

            @pl.when(place[1] == 0)
            def _():
                edge[...] = beside[:, SUBLANES - 1, :]

            @pl.when(place[1] != 0)
            def _():
                edge[...] = beside[:, 0, :]


def local_state(place, keys, values, features, with_edge):
    tile_rows, tile_cols, channels = keys.shape
    width = features.shape[2]
    rows = halves(channels)[2]
    block = pl.BlockSpec((tile_rows, tile_cols, WIDE), lambda i, c: (0, 0, i))
    shapes = [jax.ShapeDtypeStruct((rows, LANES), jnp.float32)] * 2
    scratch = [pltpu.VMEM((2, rows, LANES), jnp.float32)]
    shapes.append(pltpu.HBM((1, tile_cols, width), features.dtype))
    scratch.append(pltpu.VMEM((tile_cols, width), features.dtype))
    if with_edge:
        shapes.append(jax.ShapeDtypeStruct((tile_rows, width), features.dtype))
        scratch.append(pltpu.VMEM((tile_rows, SUBLANES, width), features.dtype))
    return pl.pallas_call(
        functools.partial(state_kernel, channels),
        out_shape=shapes,
        grid_spec=pltpu.PrefetchScalarGridSpec(
            num_scalar_prefetch=1,
            grid=(pl.cdiv(channels, WIDE),),
            in_specs=[block, block, pl.BlockSpec(memory_space=pl.ANY)],
            out_specs=[
                pl.BlockSpec(memory_space=pl.ANY if len(x.shape) == 3 else pltpu.VMEM) for x in shapes
            ],
            scratch_shapes=scratch + [pltpu.SemaphoreType.DMA((3,))],
        ),
        compiler_params=pltpu.CompilerParams(vmem_limit_bytes=8 << 20),
        cost_estimate=pl.CostEstimate(flops=1 << 29, bytes_accessed=64 << 20, transcendentals=0),
        name="local_state",
    )(place, *(pltpu.with_memory_space_constraint(x, pltpu.HBM) for x in (keys, values, features)))


def in_two(x):
    high = x.astype(jnp.bfloat16)
    return high, (x - high.astype(jnp.float32)).astype(jnp.bfloat16)


def attend_kernel(channels, place, q_ref, mine, other, ends, _, out, gated, packed, sem):
    tiles, per, rows = halves(channels)
    step = pl.program_id(0)
    core = place[0]
    tile_rows, tile_cols, _ = q_ref.shape
    tokens = tile_rows * tile_cols
    copies = [
        pltpu.make_async_copy(ends.at[k], gated.at[(tile_rows - 1) * low], sem.at[k])
        for k, low in enumerate((1 - core, core))
    ]

    @pl.when(step == 0)
    def _():
        for copy in copies:
            copy.start()
        packed[core] = mine[...]
        packed[1 - core] = other[...]

    mask = same_head(PAIR)
    lane = lax.broadcasted_iota(jnp.int32, (tokens, PAIR), 1)
    zero = jnp.zeros((), jnp.bfloat16)

    def weighted(queries, matrices):
        total = None
        for matrix in matrices:
            matrix = jnp.where(mask, matrix, zero)
            term = lax.dot_general(
                queries, matrix, (((1,), (1,)), ((), ())), preferred_element_type=jnp.float32
            )
            total = term if total is None else total + term
        return total

    for part in range(WIDE // PAIR):
        pair = step * (WIDE // PAIR) + part
        at = slice(part * PAIR, (part + 1) * PAIR)
        queries = jnp.maximum(q_ref[:, :, at].reshape(tokens, PAIR), 0)
        queries = jnp.where(lane < channels - pair * PAIR, queries, zero)
        states, totals = [], []
        for side in range(PAIR // LANES):
            tile = jnp.minimum(pair * (PAIR // LANES) + side, tiles - 1)
            half, place = tile // per, tile % per
            start = pl.multiple_of(place * HEAD_DIM, HEAD_DIM)
            states.append(packed[half, pl.ds(start, HEAD_DIM), :])
            totals.append(packed[half, pl.ds(per * HEAD_DIM + place, 1), :])
        state, total = jnp.concatenate(states, 1), jnp.concatenate(totals, 1)
        numerator = weighted(
            queries, [jnp.concatenate([x] * (PAIR // HEAD_DIM), 0) for x in in_two(state)]
        )
        denominator = weighted(queries, [jnp.broadcast_to(x, (PAIR, PAIR)) for x in in_two(total)])
        result = (numerator / (denominator + 1e-15)).astype(jnp.bfloat16)
        out[:, :, at] = result.reshape(tile_rows, tile_cols, PAIR)

    @pl.when(step == pl.num_programs(0) - 1)
    def _():
        for copy in copies:
            copy.wait()


def attend(place, queries, mine, other, ends, gated):
    tile_rows, tile_cols, channels = queries.shape
    rows = halves(channels)[2]
    block = pl.BlockSpec((tile_rows, tile_cols, WIDE), lambda i, c: (0, 0, i))
    half = pl.BlockSpec((rows, LANES), lambda i, c: (0, 0))
    anywhere = pl.BlockSpec(memory_space=pl.ANY)
    return pl.pallas_call(
        functools.partial(attend_kernel, channels),
        out_shape=[
            jax.ShapeDtypeStruct(x.shape, jnp.bfloat16) for x in (queries, gated)
        ],
        grid_spec=pltpu.PrefetchScalarGridSpec(
            num_scalar_prefetch=1,
            grid=(pl.cdiv(channels, WIDE),),
            in_specs=[block, half, half, pl.BlockSpec(memory_space=pltpu.VMEM), anywhere],
            out_specs=[block, anywhere],
            scratch_shapes=[
                pltpu.VMEM((2, rows, LANES), jnp.float32),
                pltpu.SemaphoreType.DMA((2,)),
            ],
        ),
        input_output_aliases={5: 1},
        compiler_params=pltpu.CompilerParams(vmem_limit_bytes=8 << 20),
        cost_estimate=SMALL,
        name="attend",
    )(place, queries, mine, other, ends, gated)


def widened(x):
    channel = lax.broadcasted_iota(jnp.int32, (1, x.shape[1]), 1)
    return x.astype(jnp.float32) * jnp.where(channel < x.shape[1] // 2, 1.0, 0.5)


def conv_kernel(targets, firsts, unroll, *refs):
    where, features, beside, *refs = refs
    if not targets:
        near, far, near_corner, far_corner, *refs = refs
        parts, refs = refs[: len(firsts)], refs[len(firsts) :]
        *refs, sem = refs
    weight, bias, out, *refs = refs
    copies = []
    if not targets:
        gated, *refs = refs
        for k, (start, part) in enumerate(zip(firsts, parts)):
            place = gated.at[pl.ds(start, part.shape[0])]
            copies.append(pltpu.make_async_copy(part, place, sem.at[k]))
            copies[-1].start()
    weights, biases, margins, sums, carry = refs
    tile_rows, tile_cols, channels = features.shape
    hidden = channels // 2
    tiles = pl.cdiv(hidden, LANES)
    first_gate = hidden // LANES
    shift = LANES - hidden % LANES
    count = len(targets) or 2
    last = tile_rows - 1
    core = where[0]
    if targets:
        first = targets[0] - 1
        sources = [(features, first + k) for k in range(count + 2)]
        triples = [(k, k + 1, k + 2) for k in range(count)]
        orders = [[0, 1, 2]] * count
    else:
        sources = [
            (near, 0), (features, (1 - core) * last), (features, 1 + (1 - core) * (last - 2)),
            (far, 0), (features, core * last), (features, 1 + core * (last - 2)),
        ]
        triples = [(0, 1, 2), (3, 4, 5)]
        orders = [[2 * (1 - core), 1, 2 * core], [2 * core, 1, 2 * (1 - core)]]

    for tap in range(3):
        weights[tap, :, :channels] = widened(weight[tap])
    biases[:, :channels] = widened(bias[...])
    for side in range(2):
        place = side * (beside.shape[0] - 1)
        keep = where[1 + side].astype(jnp.float32)
        edge = beside[place].astype(jnp.float32) * keep
        column = slice(2 * side, 2 * side + 1)
        if targets:
            rows = [edge[first + tap : first + tap + count] for tap in range(3)]
            margins[side, :, :channels] = sum(
                rows[tap] * weights[tap, column, :channels] for tap in range(3)
            )
            continue
        top = edge[:1], edge[1:2]
        bottom = edge[last:], edge[last - 1 : last]
        for target, corner in enumerate((near_corner, far_corner)):
            below = core == (1 if target else 0)
            rows = [corner[place : place + 1].astype(jnp.float32) * keep]
            rows += [jnp.where(below, low, high) for low, high in zip(bottom, top)]
            margins[side, target : target + 1, :channels] = sum(
                row * weights[tap, column, :channels] for row, tap in zip(rows, orders[target])
            )

    def span(tile):
        if isinstance(tile, int):
            return slice(tile * LANES, (tile + 1) * LANES)
        return pl.ds(pl.multiple_of(tile * LANES, LANES), LANES)

    def read(source, row, tile):
        if not isinstance(tile, int) or (tile + 1) * LANES <= channels:
            return source[row, :, span(tile)].astype(jnp.float32)
        part = source[row, :, tile * LANES :].astype(jnp.float32)
        fill = jnp.zeros((tile_cols, LANES - part.shape[1]), jnp.float32)
        return jnp.concatenate([part, fill], 1)

    def add_up(tile, buffer):
        at = span(tile)
        tokens = [read(source, row, tile) for source, row in sources]
        factors = [
            [[weights[tap, col : col + 1, at] for col in range(3)] for tap in order]
            for order in (orders[:1] if targets else orders)
        ]
        for target, triple in enumerate(triples):
            factor = factors[0 if targets else target]
            for col in (0, 2, 1):
                total = sum(factor[k][col] * tokens[triple[k]] for k in range(3))
                if col == 1:
                    total = total + biases[:, at]
                sums[buffer, target, col, 8 : 8 + tile_cols, :] = total
            sums[buffer, target, 0, 7:8, :] = margins[0, target : target + 1, at]
            sums[buffer, target, 2, 8 + tile_cols : 9 + tile_cols, :] = margins[1, target : target + 1, at]

    def collect(buffer, target):
        return (
            sums[buffer, target, 1, 8 : 8 + tile_cols, :]
            + sums[buffer, target, 0, 7 : 7 + tile_cols, :]
            + sums[buffer, target, 2, 9 : 9 + tile_cols, :]
        )

    def gate(buffer, target):
        x = collect(buffer, target)
        return pltpu.roll(x + x * jnp.tanh(x), shift, 1)

    lane = lax.broadcasted_iota(jnp.int32, (tile_cols, LANES), 1)

    def add_both(tile, step):
        add_up(tile + first_gate + 1, 2 * step)
        add_up(tile, 2 * step + 1)

    def finish(tile, step, before):
        at = span(tile)
        result = []
        for target in range(count):
            after = gate(2 * step, target)
            factor = jnp.where(lane < shift, before[target], after)
            product = (collect(2 * step + 1, target) * factor).astype(jnp.bfloat16)
            if isinstance(tile, int):
                size = min(hidden - tile * LANES, LANES)
                out[target, :, tile * LANES : tile * LANES + size] = product[:, :size]
            else:
                out[target, :, at] = product
            result.append(after)
        return result

    add_up(first_gate, 0)
    for target in range(count):
        carry[target] = gate(0, target)
    add_both(0, 0)

    full = tiles // unroll - 1

    @pl.loop(0, full)
    def _(i):
        before = [carry[target] for target in range(count)]
        for step in range(unroll):
            tile = i * unroll + step
            add_both(tile + 1, (step + 1) % unroll)
            before = finish(tile, step, before)
        for target in range(count):
            carry[target] = before[target]

    before = [carry[target] for target in range(count)]
    for tile in range(full * unroll, tiles):
        if tile + 1 < tiles:
            add_both(tile + 1, (tile + 1) % unroll)
        before = finish(tile, tile % unroll, before)

    for copy in copies:
        copy.wait()


def conv(targets, where, features, beside, halos, parts, firsts, weight, bias):
    tile_rows, tile_cols, channels = features.shape
    hidden = channels // 2
    count = len(targets) or 2
    unroll = 2 if targets else 4
    padded = pl.cdiv(channels, LANES) * LANES
    whole = pl.BlockSpec(memory_space=pltpu.VMEM)
    operands = [features, beside, *halos, *parts, weight, bias]
    shapes = [jax.ShapeDtypeStruct((count, tile_cols, hidden), jnp.bfloat16)]
    specs = [whole]
    scratch = [
        pltpu.VMEM((3, 3, padded), jnp.float32),
        pltpu.VMEM((1, padded), jnp.float32),
        pltpu.VMEM((2, count, padded), jnp.float32),
        pltpu.VMEM((2 * unroll, count, 3, tile_cols + 16, LANES), jnp.float32),
        pltpu.VMEM((count, tile_cols, LANES), jnp.float32),
    ]
    if not targets:
        shapes.append(jax.ShapeDtypeStruct((tile_rows, tile_cols, hidden), jnp.bfloat16))
        specs.append(pl.BlockSpec(memory_space=pl.ANY))
        scratch.append(pltpu.SemaphoreType.DMA((len(parts),)))
    return pl.pallas_call(
        functools.partial(conv_kernel, targets, firsts, unroll),
        out_shape=shapes,
        in_specs=[pl.BlockSpec(memory_space=pltpu.SMEM)] + [whole] * len(operands),
        out_specs=specs,
        scratch_shapes=scratch,
        compiler_params=pltpu.CompilerParams(vmem_limit_bytes=8 << 20),
        cost_estimate=SMALL,
        name="conv_rows" if targets else "conv_ends",
    )(where, *operands)


def near_kernel(place, features, near, sem):
    row = (features.shape[0] - 1) * (1 - place[0])
    copy = pltpu.make_async_copy(features.at[pl.ds(row, 1)], near, sem)
    copy.start()
    copy.wait()


def near_row(place, features):
    return pl.pallas_call(
        near_kernel,
        out_shape=pltpu.HBM((1, *features.shape[1:]), features.dtype),
        in_specs=[pl.BlockSpec(memory_space=pltpu.SMEM), pl.BlockSpec(memory_space=pltpu.VMEM)],
        out_specs=pl.BlockSpec(memory_space=pl.ANY),
        scratch_shapes=[pltpu.SemaphoreType.DMA],
        compiler_params=pltpu.CompilerParams(vmem_limit_bytes=8 << 20),
        cost_estimate=SMALL,
        name="near_row",
    )(place, features)


def swap(axis, bit):
    return [(i, i ^ bit) for i in range(lax.axis_size(axis))]


def together(*values):
    return lax.optimization_barrier(values)


def on_device(queries, keys, values, features, conv_weight, conv_bias):
    tile_rows, tile_cols, channels = features.shape
    rows, cols = lax.axis_size("row"), lax.axis_size("col")
    row, col = lax.axis_index("row"), lax.axis_index("col")
    core = (row % 2).astype(jnp.int32)
    place = jnp.stack([core, col]).astype(jnp.int32)
    where = jnp.stack([core, col > 0, col < cols - 1]).astype(jnp.int32)
    bias = conv_bias.reshape(1, -1)
    next_chip = [(i, i + 1) for i in range(1, rows - 1, 2)]
    next_chip += [(i + 1, i) for i, _ in next_chip]

    mine, other, far, *edges = local_state(place, keys, values, features, cols == 2)
    total = mine + lax.ppermute(other, "row", swap("row", 1))
    if cols == 2:
        beside = lax.ppermute(edges[0], "col", swap("col", 1))[None]
    else:
        right = [(i, i + 1) for i in range(cols - 1)]
        left = [(i + 1, i) for i in range(cols - 1)]
        beside = jnp.stack(
            [
                lax.ppermute(features[:, -1], "col", right),
                lax.ppermute(features[:, 0], "col", left),
            ]
        )
    rounds = [("row", 1 << k) for k in range(2, (rows - 1).bit_length())]
    rounds[1:1] = [("col", 1 << k) for k in range((cols - 1).bit_length())]
    rounds.append(("row", 2))
    mixed = {0: (4, 2), len(rounds) - 1: (2, 4)}
    middle = min(4, tile_rows - 1)
    work = [tuple(range(1, middle)), tuple(range(middle, tile_rows - 1)), ()]
    firsts, parts = [], []

    def next_work(given):
        targets = work.pop(0)
        halos = () if targets else (near_halo, far_halo, near_corner, far_corner)
        earlier = () if targets else tuple(parts)
        made = list(
            conv(targets, given, features, beside, halos, earlier, tuple(firsts), conv_weight, bias)
        )
        if not targets:
            return made
        firsts.append(targets[0])
        parts.extend(made)
        return made

    for turn, (axis, bit) in enumerate(rounds):
        pairs = swap(axis, bit)
        if turn in mixed:
            pairs = [(i, i ^ mixed[turn][i % 2]) for i in range(rows)]
        received = lax.ppermute(total, axis, pairs)
        if turn == 0:
            far_halo = lax.ppermute(together(far, total)[0], "row", next_chip)
            near = near_row(together(place, total)[0], features)
            received, near, beside = together(received, near, beside)
            near_halo = lax.ppermute(near, "row", swap("row", 1))
            near_corner = jnp.where(core == 0, beside[:, -1], beside[:, 0])
            far_corner = jnp.where(core == 0, beside[:, 0], beside[:, -1])
            near_corner = lax.ppermute(near_corner, "row", swap("row", 1))
            far_corner = lax.ppermute(far_corner, "row", next_chip)
        if turn == 1:
            received, near_halo, near_corner = together(received, near_halo, near_corner)
        if turn > 0 and work:
            made = next_work(together(where, total)[0])
            received, made[0] = together(received, made[0])
            if work:
                parts[-1] = made[0]
        if turn == 2:
            received, far_halo, far_corner = together(received, far_halo, far_corner)
        total = total + received
    rest = lax.ppermute(total, "row", swap("row", 1))
    while work:
        made = next_work(where)
    return tuple(attend(place, queries, total, rest, *made))


def solution(mesh):
    tiled = P("row", "col", None)
    return jax.shard_map(
        on_device,
        mesh=mesh,
        in_specs=(tiled, tiled, tiled, tiled, P(), P()),
        out_specs=(tiled, tiled),
        check_vma=False,
    )
```
